512 devices in a mesh: tiles: 128 (over z, y, core), bands: 4 (over x).
Axes of the slice: x: 4, y: 8, z: 8, core: 2. Of those that a mesh axis runs over, the one named last changes fastest.
Arguments:
- view_tiles: bfloat16 [12288, 128, 128], P('tiles'), may hold values from 0 to 0.11111111
- vis_rows: int32 [12288], P('tiles'), may hold values from 0 to 2047, as said below
- vis_cols: int32 [12288], P('tiles'), may hold values from 0 to 2047, as said below
- seed_grad: float32 [48, 262144], P('bands', 'tiles'), may hold values from 0.3 to 3
- emissivity: float32 [262144], P('tiles'), may hold values from 0.2 to 0.9
- emissive_power: float32 [48, 262144], P('bands', 'tiles'), may hold values from 0.3 to 4.5
- irradiance: float32 [48, 262144], P('bands', 'tiles'), may hold values from 0.1 to 1
Outputs:
- adjoint: float32 [48, 262144], P('bands', 'tiles')
- emis_grad: float32 [262144], P('tiles')
The draws below stay inside these ranges and needn't reach their ends.
Inputs may be any that keep to these rules, and one draw needn't show every extreme that they name: `vis_rows`: block k's row tile is owned by the index of tiles that holds block k: it lies from (k // 96) * 16 to (k // 96 + 1) * 16 - 1. `vis_cols`: tile t is owned by index t // 16 of tiles. Among the 96 blocks held by one index of tiles, at most 2 have column tiles owned by any one index; in every draw one index of tiles is named by exactly 2 blocks of every index.
All inputs are finite; a program needn't handle non-finite values.
Results may differ from the reference program's by a relative error of at most 0.00045.
Values may be sent and summed in bfloat16 or wider, within the bound.
A program may use at most 64 MiB of HBM per device.

```python
import jax
import jax.numpy as jnp
from jax import lax

PATCH = 128
BANDS = 48
TILES_DEV = 16
VIS = 6
ITERS = 2
BLK_DEV = 96
CAP = 2
PATCHES = 262144
BLOCKS = 12288
N_TILES = 128


def draw_view_tiles(key, part):
    height = 1.0 / (3.0 * VIS)
    unit = jax.random.uniform(jax.random.fold_in(key, 3), (BLOCKS, PATCH, PATCH), jnp.float32)
    row_pos = jnp.arange(PATCH, dtype=jnp.int32)[:, None]
    col_pos = jnp.arange(PATCH, dtype=jnp.int32)[None, :]
    gap = jnp.abs(row_pos - col_pos)
    center = (1.0 + 0.99 * unit) * height
    beside = 0.5 * unit * height
    distant = 0.01 * unit * height
    value = jnp.where(gap == 0, center, jnp.where(gap == 1, beside, distant))
    return value.astype(jnp.bfloat16)


def draw_seed_grad(key, part):
    unit = jax.random.uniform(jax.random.fold_in(key, 5), (BANDS, PATCHES), jnp.float32)
    value = 0.3 * jnp.exp(unit * jnp.log(10.0))
    return jnp.clip(value, 0.3, 3.0)


def draw_vis_rows(key, part):
    owners = jnp.arange(BLOCKS, dtype=jnp.int32) // BLK_DEV
    local_tiles = jax.random.randint(key, (BLOCKS,), 0, TILES_DEV, dtype=jnp.int32)
    return owners * TILES_DEV + local_tiles


def draw_vis_cols(key, part):
    slot_total = N_TILES * CAP
    favored = jax.random.randint(jax.random.fold_in(key, 7), (), 0, N_TILES, dtype=jnp.int32)

    def one_owner(owner_key):
        shuffled = jax.random.permutation(jax.random.fold_in(owner_key, 1), slot_total)
        slot_owner = shuffled // CAP
        ranking = jnp.where(slot_owner == favored, -1, jnp.arange(slot_total, dtype=jnp.int32))
        arranged = shuffled[jnp.argsort(ranking, stable=True)]
        chosen = arranged[:BLK_DEV]
        chosen = chosen[jax.random.permutation(jax.random.fold_in(owner_key, 2), BLK_DEV)]
        target = (chosen // CAP).astype(jnp.int32)
        local_tiles = jax.random.randint(jax.random.fold_in(owner_key, 3), (BLK_DEV,), 0, TILES_DEV, dtype=jnp.int32)
        return target * TILES_DEV + local_tiles
    owner_keys = jax.random.split(jax.random.fold_in(key, 11), N_TILES)
    return jax.vmap(one_owner)(owner_keys).reshape(BLOCKS).astype(jnp.int32)


def draw_emissive_power(key, part):
    ramp = 1.0 + 2.0 * jnp.arange(BANDS, dtype=jnp.float32)[:, None] / (BANDS - 1)
    unit = jax.random.uniform(key, (BANDS, PATCHES), jnp.float32)
    base = 0.3 + 1.2 * unit
    return base * ramp


def block_scale(key, extent, pieces, low, high):
    loudness = 1.0
    for dim, shards_of in pieces:
        heights = jax.random.uniform(jax.random.fold_in(jax.random.fold_in(key, 6), dim), (shards_of,), jnp.float32, low / len(pieces), high / len(pieces))
        loudness = loudness * jnp.repeat(jnp.exp(heights), extent[dim] // shards_of).reshape((-1,) + (1,) * (len(extent) - 1 - dim))
    return loudness


def setup_inputs(seed: int = 0) -> dict:
    key_list = jax.random.split(jax.random.key(seed), 8)
    return {
        "view_tiles": draw_view_tiles(jax.random.fold_in(key_list[7], 71), 0),
        "vis_rows": draw_vis_rows(jax.random.fold_in(key_list[7], 71), 0),
        "vis_cols": draw_vis_cols(jax.random.fold_in(key_list[7], 71), 0),
        "seed_grad": draw_seed_grad(jax.random.fold_in(key_list[7], 71), 0),
        "emissivity": jnp.clip(0.2 + 0.7 * jax.random.uniform(key_list[4], (PATCHES,), jnp.float32) ** block_scale(key_list[4], (PATCHES,), ((0, 128),), -0.2, 0.2), 0.2, 0.9),
        "emissive_power": draw_emissive_power(jax.random.fold_in(key_list[7], 71), 0),
        "irradiance": jnp.clip(0.1 + 0.9 * jax.random.uniform(key_list[6], (BANDS, PATCHES), jnp.float32) ** block_scale(key_list[6], (BANDS, PATCHES), ((0, 4), (1, 128)), -0.2, 0.2), 0.1, 1.0),
    }


def reference(view_tiles, vis_rows, vis_cols, seed_grad, emissivity, emissive_power, irradiance):
    tile_total = emissivity.shape[0] // PATCH
    reflect = (1.0 - emissivity).reshape(tile_total, PATCH)
    seed_tiles = seed_grad.reshape(BANDS, tile_total, PATCH)
    tile_groups = view_tiles.reshape(N_TILES, BLK_DEV, PATCH, PATCH)
    row_groups = vis_rows.reshape(N_TILES, BLK_DEV).astype(jnp.int32)
    col_groups = vis_cols.reshape(N_TILES, BLK_DEV).astype(jnp.int32)
    adjoint = seed_tiles
    for sweep_index in range(ITERS):
        scaled = (reflect[None] * adjoint).astype(jnp.bfloat16)

        def add_group(total, group):
            group_tiles, group_rows, group_cols = group
            picked = scaled[:, group_rows, :].astype(jnp.float32)
            block_terms = jnp.einsum("bkp,kpq->bkq", picked, group_tiles.astype(jnp.float32),
                                     precision=lax.Precision.HIGHEST)
            return total.at[:, group_cols, :].add(block_terms), None

        incoming, unused = lax.scan(add_group, jnp.zeros((BANDS, tile_total, PATCH), jnp.float32),
                                    (tile_groups, row_groups, col_groups))
        adjoint = seed_tiles + incoming
    adjoint_flat = adjoint.reshape(BANDS, tile_total * PATCH)
    contrast = emissive_power - irradiance
    emis_grad = jnp.sum(adjoint_flat * contrast, axis=0) / BANDS
    return adjoint_flat, emis_grad
```

```python
import functools

import jax
import jax.numpy as jnp
from jax import lax
from jax.experimental import pallas as pl
from jax.experimental.pallas import tpu as pltpu
from jax.sharding import PartitionSpec as P

BANDS = 48
ITERS = 2
PATCH = 128
CAP = 2
CORES = 2
PAIRS = 2
F32, BF16 = jnp.float32, jnp.bfloat16
MESH = pl.DeviceIdType.MESH


def far_first(n):
    out = []
    for d in range(n // 2, 0, -1):
        out.append(d)
        if n - d != d:
            out.append(n - d)
    return out


def kernel(dims, *refs):
    nz, ny, nx = dims
    (view_hbm, rows_ref, cols_ref, seed_ref, emis_ref, power_ref, irr_ref,
     adj_ref, grad_ref,
     view, scaled, terms, prev, pick, select, sum_rows, mid_rest, acc,
     meta_send, meta_recv, s1_send, s1_recv, s2_send, s2_recv, g_part, g_recv,
     view_sem, meta_ss, meta_rs, s1_ss, s1_rs, s2_ss, s2_rs, g_ss, g_rs) = refs
    nblk = view.shape[0]
    bands, width = seed_ref.shape
    tiles = width // PATCH
    bp = bands // PAIRS
    hb = bp // 2
    me = lax.axis_index("tiles")
    my_x = lax.axis_index("bands")
    my_c = lax.rem(me, CORES)
    my_y = lax.rem(me // CORES, ny)
    my_z = me // (CORES * ny)
    ring = (ny, nz)
    ring2 = (nz, ny)
    mine = (my_y, my_z)
    mine2 = (my_z, my_y)

    def index_of(kind, first, second, core):
        y, z = (first, second) if kind == 0 else (second, first)
        return (z * ny + y) * CORES + core

    peers1, peers2 = [], []
    for kind in (0, 1):
        p1, p2 = [], []
        for off in far_first(ring[kind]) + [0]:
            for dc in range(CORES):
                if off == 0 and dc == 0:
                    continue
                pos = lax.rem(mine[kind] + off, ring[kind])
                core = lax.rem(my_c + dc, CORES)
                p1.append((kind, pos, core, index_of(kind, pos, mine2[kind], core), off, dc))
        for off in far_first(ring2[kind]):
            pos = lax.rem(mine2[kind] + off, ring2[kind])
            p2.append((kind, pos, index_of(kind, mine[kind], pos, my_c)))
        peers1.append(p1)
        peers2.append(p2)

    def interleave(a, b):
        out = []
        for i in range(max(len(a), len(b))):
            out += a[i:i + 1] + b[i:i + 1]
        return out

    order1 = interleave(*peers1)
    order2 = interleave(*peers2)
    x_peers = [lax.rem(my_x + off, nx) for off in range(1, nx)]

    view_copy = pltpu.make_async_copy(view_hbm, view, view_sem)
    view_copy.start()
    barrier = pltpu.get_barrier_semaphore()
    met = 0
    for kind, pos, core, dev, off, dc in order1:
        if kind == 1 and off == 0:
            continue
        pl.semaphore_signal(barrier, inc=1, device_id={"tiles": dev}, device_id_type=MESH)
        met += 1
    for x in x_peers:
        pl.semaphore_signal(barrier, inc=1, device_id={"bands": x}, device_id_type=MESH)
        met += 1

    col_row = cols_ref[...]
    lane = lax.broadcasted_iota(jnp.int32, (nblk, nblk), 1)
    sub = lax.broadcasted_iota(jnp.int32, (nblk, nblk), 0)
    spread = jnp.broadcast_to(col_row, (nblk, nblk))
    col_col = jnp.sum(jnp.where(lane == sub, spread, 0).astype(F32), axis=1, keepdims=True).astype(jnp.int32)
    tgt_row = lax.shift_right_logical(spread, tiles.bit_length() - 1)
    tgt_col = lax.shift_right_logical(jnp.broadcast_to(col_col, (nblk, nblk)), tiles.bit_length() - 1)
    same = tgt_row == tgt_col
    rank_row = jnp.sum(jnp.where(same & (sub < lane), 1.0, 0.0), axis=0, keepdims=True).astype(jnp.int32)
    rank_col = jnp.sum(jnp.where(same & (lane < sub), 1.0, 0.0), axis=1, keepdims=True).astype(jnp.int32)
    tb = tiles.bit_length() - 1
    cb = CORES.bit_length() - 1
    yb = ny.bit_length() - 1

    def place(cols, rank, kind):
        tile = cols & (tiles - 1)
        core = lax.shift_right_logical(cols, tb) & (CORES - 1)
        y = lax.shift_right_logical(cols, tb + cb) & (ny - 1)
        z = lax.shift_right_logical(cols, tb + cb + yb)
        first, second = (y, z) if kind == 0 else (z, y)
        slots = ring2[kind] * CAP
        return (first * CORES + core) * slots + second * CAP + rank, second * tiles + tile

    for kind in (0, 1):
        n1 = ring[kind] * CORES
        slots = ring2[kind] * CAP
        pos_row, _ = place(col_row, rank_row, kind)
        pos_col, id_col = place(col_col, rank_col, kind)
        slot_no = lax.broadcasted_iota(jnp.int32, (n1 * slots, nblk), 0)
        pick[kind] = jnp.where(slot_no == pos_row, 1.0, 0.0).astype(BF16)
        lane_slot = lax.broadcasted_iota(jnp.int32, (nblk, PATCH), 1) & (slots - 1)
        id_value = (id_col + 1).astype(F32)
        pos_wide = jnp.broadcast_to(pos_col, (nblk, PATCH)) - lane_slot
        for q in range(n1):
            hit = jnp.where(pos_wide == q * slots, id_value, 0.0)
            meta_send[kind, q] = jnp.sum(hit, axis=0, keepdims=True) - 1.0

    def scale(p, first):
        lo = p * bp
        for t in range(tiles):
            lanes = slice(t * PATCH, (t + 1) * PATCH)
            adj = seed_ref[lo:lo + bp, lanes]
            if not first:
                adj = adj + acc[p, pl.ds(t, bp, stride=tiles), :]
            scaled[p, t, 0:bp, :] = ((1.0 - emis_ref[0:1, lanes]) * adj).astype(BF16)

    def products(p):
        group = 24

        def body(step, carry):
            base = step * group
            for j in range(0, group, 2):
                k = base + j
                r0 = rows_ref[k] & (tiles - 1)
                r1 = rows_ref[k + 1] & (tiles - 1)
                left = jnp.concatenate([scaled[p, r0], scaled[p, r1]], axis=0)
                right = jnp.concatenate([view[k], view[k + 1]], axis=1)
                out = jnp.dot(left, right, preferred_element_type=F32)
                n = scaled.shape[2]
                terms[p, pl.ds(k, bp, stride=nblk), :] = out[0:bp, 0:PATCH]
                terms[p, pl.ds(k + 1, bp, stride=nblk), :] = out[n:n + bp, PATCH:2 * PATCH]
            return carry

        lax.fori_loop(0, nblk // group, body, 0)

    def choose(it, p):
        for j in range(bp):
            kind, jb = divmod(j, hb)
            rows = slice(j * nblk, (j + 1) * nblk)
            value = terms[p, rows, :]
            if it == 0:
                value = value.astype(BF16)
                prev[p, rows, :] = value
            else:
                value = (value - prev[p, rows, :].astype(F32)).astype(BF16)
            n1 = ring[kind] * CORES
            slots = ring2[kind] * CAP
            out = jnp.dot(pick[kind], value, preferred_element_type=F32).astype(BF16)
            s1_send[it, p, kind, :, jb] = out.reshape(n1, slots, PATCH)
        for kind in (0, 1):
            own = mine[kind] * CORES + my_c
            s1_recv[it, p, kind, own] = s1_send[it, p, kind, own]

    def send1(it, p):
        for kind, pos, core, dev, off, dc in order1:
            pltpu.make_async_remote_copy(
                src_ref=s1_send.at[it, p, kind, pos * CORES + core],
                dst_ref=s1_recv.at[it, p, kind, mine[kind] * CORES + my_c],
                send_sem=s1_ss.at[it, p, kind], recv_sem=s1_rs.at[it, p, kind],
                device_id={"tiles": dev}, device_id_type=MESH).start()

    def wait1(it, p, kind):
        n1 = ring[kind] * CORES
        ref = s1_recv.at[it, p, kind, 0:n1 - 1]
        pltpu.make_async_copy(ref, ref, s1_rs.at[it, p, kind]).wait()

    def send_meta():
        for kind, pos, core, dev, off, dc in order1:
            pltpu.make_async_remote_copy(
                src_ref=meta_send.at[kind, pos * CORES + core],
                dst_ref=meta_recv.at[kind, mine[kind] * CORES + my_c],
                send_sem=meta_ss.at[kind], recv_sem=meta_rs.at[kind],
                device_id={"tiles": dev}, device_id_type=MESH).start()

    def take_meta(kind):
        n1 = ring[kind] * CORES
        slots = ring2[kind] * CAP
        own = mine[kind] * CORES + my_c
        ref = meta_recv.at[kind, 0:n1 - 1]
        pltpu.make_async_copy(ref, ref, meta_rs.at[kind]).wait()
        meta_recv[kind, own] = meta_send[kind, own]
        per = PATCH // slots
        rows = ring2[kind] * tiles
        part = lax.broadcasted_iota(jnp.int32, (1, PATCH), 1) // slots
        row_no = lax.broadcasted_iota(jnp.int32, (rows, PATCH), 0).astype(F32)
        for h in range(n1 // per):
            ids = jnp.zeros((1, PATCH), F32)
            for j in range(per):
                ids = jnp.where(part == j, meta_recv[kind, h * per + j], ids)
            select[kind, :, h * PATCH:(h + 1) * PATCH] = jnp.where(row_no == ids, 1.0, 0.0).astype(BF16)

    def middle(it, p, kind):
        n1 = ring[kind] * CORES
        n2 = ring2[kind]
        slots = n2 * CAP
        for jb in range(hb):
            got = s1_recv[it, p, kind, :, jb].reshape(n1 * slots, PATCH)
            total = jnp.dot(select[kind], got, preferred_element_type=F32)
            if it > 0:
                total = total + mid_rest[p, kind, jb]
            out = total.astype(BF16)
            if it < ITERS - 1:
                mid_rest[p, kind, jb] = total - out.astype(F32)
            s2_send[it, p, kind, :, jb] = out.reshape(n2, tiles, PATCH)
        own = mine2[kind]
        s2_recv[it, p, kind, own] = s2_send[it, p, kind, own]

    def send2(it, p, kinds):
        for kind, pos, dev in order2:
            if kind in kinds:
                pltpu.make_async_remote_copy(
                    src_ref=s2_send.at[it, p, kind, pos],
                    dst_ref=s2_recv.at[it, p, kind, mine2[kind]],
                    send_sem=s2_ss.at[it, p, kind], recv_sem=s2_rs.at[it, p, kind],
                    device_id={"tiles": dev}, device_id_type=MESH).start()

    def finish(it, p):
        for kind in (0, 1):
            n2 = ring2[kind]
            ref = s2_recv.at[it, p, kind, 0:n2 - 1]
            pltpu.make_async_copy(ref, ref, s2_rs.at[it, p, kind]).wait()
            for jb in range(hb):
                total = s2_recv[it, p, kind, 0, jb].astype(F32)
                for j in range(1, n2):
                    total = total + s2_recv[it, p, kind, j, jb].astype(F32)
                row = (kind * hb + jb) * tiles
                if it > 0:
                    total = total + acc[p, row:row + tiles, :]
                acc[p, row:row + tiles, :] = total

    if scaled.shape[2] > bp:
        pad = scaled.shape[2] - bp
        for p in range(PAIRS):
            scaled[p, :, bp:, :] = jnp.zeros((tiles, pad, PATCH), BF16)
    for p in range(PAIRS):
        scale(p, True)
    view_copy.wait()
    for it in range(ITERS):
        for p in range(PAIRS):
            if it > 0:
                finish(it - 1, p)
                scale(p, False)
            products(p)
            choose(it, p)
            if it == 0 and p == 0:
                pl.semaphore_wait(barrier, met)
            send1(it, p)
            if it == 0 and p == 0:
                send_meta()
        for p in range(PAIRS):
            if it == 0 and p == 0:
                take_meta(0)
                take_meta(1)
            for kind in (0, 1):
                wait1(it, p, kind)
                middle(it, p, kind)
                send2(it, p, (kind,))

    for p in range(PAIRS):
        finish(ITERS - 1, p)
        lo = p * bp
        for t in range(tiles):
            lanes = slice(t * PATCH, (t + 1) * PATCH)
            adj = seed_ref[lo:lo + bp, lanes] + acc[p, pl.ds(t, bp, stride=tiles), :]
            adj_ref[lo:lo + bp, lanes] = adj
            contrast = power_ref[lo:lo + bp, lanes] - irr_ref[lo:lo + bp, lanes]
            part = jnp.sum(adj * contrast, axis=0, keepdims=True)
            if p > 0:
                part = part + g_part[t:t + 1, :]
            g_part[t:t + 1, :] = part
    for i, x in enumerate(x_peers):
        pltpu.make_async_remote_copy(
            src_ref=g_part, dst_ref=g_recv.at[i], send_sem=g_ss, recv_sem=g_rs,
            device_id={"bands": x}, device_id_type=MESH).start()
    for kind in (0, 1):
        n1 = ring[kind] * CORES
        n2 = ring2[kind]
        ref = meta_send.at[kind, 0:n1 - 1]
        pltpu.make_async_copy(ref, ref, meta_ss.at[kind]).wait()
        for it in range(ITERS):
            for p in range(PAIRS):
                ref = s1_send.at[it, p, kind, 0:n1 - 1]
                pltpu.make_async_copy(ref, ref, s1_ss.at[it, p, kind]).wait()
                ref = s2_send.at[it, p, kind, 0:n2 - 1]
                pltpu.make_async_copy(ref, ref, s2_ss.at[it, p, kind]).wait()
    pltpu.make_async_copy(g_recv, g_recv, g_rs).wait()
    total = g_part[...]
    for i in range(nx - 1):
        total = total + g_recv[i]
    grad_ref[...] = total * (1.0 / BANDS)
    pltpu.make_async_copy(g_recv, g_recv, g_ss).wait()


def local(dims, view_tiles, vis_rows, vis_cols, seed_grad, emissivity, emissive_power, irradiance):
    nz, ny, nx = dims
    nblk = view_tiles.shape[0]
    bands, width = seed_grad.shape
    tiles = width // PATCH
    bp = bands // PAIRS
    hb = bp // 2
    rp = -(-bp // 8) * 8
    n1, n2 = ny * CORES, nz
    slots = n2 * CAP
    vmem = pl.BlockSpec(memory_space=pltpu.VMEM)
    dma = pltpu.SemaphoreType.DMA
    adjoint, grad = pl.pallas_call(
        functools.partial(kernel, dims),
        out_shape=(jax.ShapeDtypeStruct((bands, width), F32), jax.ShapeDtypeStruct((tiles, PATCH), F32)),
        in_specs=[pl.BlockSpec(memory_space=pl.ANY), pl.BlockSpec(memory_space=pltpu.SMEM)] + [vmem] * 5,
        out_specs=(vmem, vmem),
        scratch_shapes=[
            pltpu.VMEM((nblk, PATCH, PATCH), BF16),
            pltpu.VMEM((PAIRS, tiles, rp, PATCH), BF16),
            pltpu.VMEM((PAIRS, bp * nblk, PATCH), F32),
            pltpu.VMEM((PAIRS, bp * nblk, PATCH), BF16),
            pltpu.VMEM((2, n1 * slots, nblk), BF16),
            pltpu.VMEM((2, n2 * tiles, n1 * slots), BF16),
            pltpu.VMEM((8, PATCH), F32),
            pltpu.VMEM((PAIRS, 2, hb, n2 * tiles, PATCH), F32),
            pltpu.VMEM((PAIRS, bp * tiles, PATCH), F32),
            pltpu.VMEM((2, n1, 1, PATCH), F32),
            pltpu.VMEM((2, n1, 1, PATCH), F32),
            pltpu.VMEM((ITERS, PAIRS, 2, n1, hb, slots, PATCH), BF16),
            pltpu.VMEM((ITERS, PAIRS, 2, n1, hb, slots, PATCH), BF16),
            pltpu.VMEM((ITERS, PAIRS, 2, n2, hb, tiles, PATCH), BF16),
            pltpu.VMEM((ITERS, PAIRS, 2, n2, hb, tiles, PATCH), BF16),
            pltpu.VMEM((tiles, PATCH), F32),
            pltpu.VMEM((nx - 1, tiles, PATCH), F32),
            dma,
            dma((2,)), dma((2,)),
            dma((ITERS, PAIRS, 2)), dma((ITERS, PAIRS, 2)),
            dma((ITERS, PAIRS, 2)), dma((ITERS, PAIRS, 2)),
            dma, dma,
        ],
        compiler_params=pltpu.CompilerParams(
            collective_id=0, has_side_effects=True, vmem_limit_bytes=40 * 2**20),
    )(view_tiles, vis_rows, vis_cols.reshape(1, nblk), seed_grad, emissivity.reshape(1, width),
      emissive_power, irradiance)
    return adjoint, grad.reshape(width)


def solution(mesh):
    placed = (
        P("tiles", None, None),
        P("tiles"),
        P("tiles"),
        P("bands", "tiles"),
        P("tiles"),
        P("bands", "tiles"),
        P("bands", "tiles"),
    )
    side = 1
    while side * side * CORES < mesh.shape["tiles"]:
        side *= 2
    dims = (mesh.shape["tiles"] // (CORES * side), side, mesh.shape["bands"])
    return jax.shard_map(
        functools.partial(local, dims),
        mesh=mesh,
        in_specs=placed,
        out_specs=(P("bands", "tiles"), P("tiles")),
        check_vma=False,
    )
```

```python
import functools

import jax
import jax.numpy as jnp
from jax import lax
from jax.experimental import pallas as pl
from jax.experimental.pallas import tpu as pltpu
from jax.sharding import PartitionSpec as P

BANDS = 48
ITERS = 2
PATCH = 128
CAP = 2
CORES = 2
PAIRS = 3
GROUP = 24
F32, BF16 = jnp.float32, jnp.bfloat16
MESH = pl.DeviceIdType.MESH


def far_first(n):
    out = []
    for d in range(n // 2, 0, -1):
        out.append(d)
        if n - d != d:
            out.append(n - d)
    return out


def kernel(dims, *refs):
    nz, ny, nx = dims
    (view_hbm, rows_hbm, cols_hbm, seed_hbm, emis_hbm, power_hbm, irr_hbm,
     adj_ref, grad_ref,
     view, rows_ref, cols_ref, seed_ref, emis_ref, power_ref, irr_ref,
     scaled, terms, prev, pick, select, mid_rest, acc,
     meta_send, meta_recv, s1_send, s1_recv, s2_send, s2_recv, g_part, g_recv,
     in_sems, view_sems, meta_ss, meta_rs, s1_ss, s1_rs, s2_ss, s2_rs, g_ss, g_rs) = refs
    nblk = view.shape[0]
    bands, width = seed_ref.shape
    tiles = width // PATCH
    bp = bands // PAIRS
    hb = bp // 2
    me = lax.axis_index("tiles")
    my_x = lax.axis_index("bands")
    my_c = lax.rem(me, CORES)
    my_y = lax.rem(me // CORES, ny)
    my_z = me // (CORES * ny)
    ring = (ny, nz)
    ring2 = (nz, ny)
    mine = (my_y, my_z)
    mine2 = (my_z, my_y)

    def index_of(kind, first, second, core):
        y, z = (first, second) if kind == 0 else (second, first)
        return (z * ny + y) * CORES + core

    peers1, peers2 = [], []
    for kind in (0, 1):
        p1, p2 = [], []
        for off in far_first(ring[kind]) + [0]:
            for dc in range(CORES):
                if off == 0 and dc == 0:
                    continue
                pos = lax.rem(mine[kind] + off, ring[kind])
                core = lax.rem(my_c + dc, CORES)
                p1.append((kind, pos, core, index_of(kind, pos, mine2[kind], core), off, dc))
        for off in far_first(ring2[kind]):
            pos = lax.rem(mine2[kind] + off, ring2[kind])
            p2.append((kind, pos, index_of(kind, mine[kind], pos, my_c)))
        peers1.append(p1)
        peers2.append(p2)

    def interleave(a, b):
        out = []
        for i in range(max(len(a), len(b))):
            out += a[i:i + 1] + b[i:i + 1]
        return out

    order1 = interleave(*peers1)
    order2 = interleave(*peers2)
    x_peers = [lax.rem(my_x + off, nx) for off in range(1, nx)]

    cols_in, rows_in, seed_in, emis_in, power_in, irr_in = [
        pltpu.make_async_copy(src, dst, in_sems.at[i]) for i, (src, dst) in enumerate((
            (cols_hbm, cols_ref), (rows_hbm, rows_ref), (seed_hbm, seed_ref), (emis_hbm, emis_ref),
            (power_hbm, power_ref), (irr_hbm, irr_ref)))]

    def view_in(step):
        part = pl.ds(step * GROUP, GROUP)
        return pltpu.make_async_copy(view_hbm.at[part], view.at[part], view_sems.at[step])

    for copy in (cols_in, rows_in, seed_in, emis_in):
        copy.start()
    for step in range(nblk // GROUP):
        view_in(step).start()
    power_in.start()
    irr_in.start()
    barrier = pltpu.get_barrier_semaphore()
    met = 0
    for kind, pos, core, dev, off, dc in order1:
        if kind == 1 and off == 0:
            continue
        pl.semaphore_signal(barrier, inc=1, device_id={"tiles": dev}, device_id_type=MESH)
        met += 1
    for x in x_peers:
        pl.semaphore_signal(barrier, inc=1, device_id={"bands": x}, device_id_type=MESH)
        met += 1

    cols_in.wait()
    col_row = cols_ref[...]
    lane = lax.broadcasted_iota(jnp.int32, (nblk, nblk), 1)
    sub = lax.broadcasted_iota(jnp.int32, (nblk, nblk), 0)
    spread = jnp.broadcast_to(col_row, (nblk, nblk))
    col_col = jnp.sum(jnp.where(lane == sub, spread, 0).astype(F32), axis=1, keepdims=True).astype(jnp.int32)
    tgt_row = lax.shift_right_logical(spread, tiles.bit_length() - 1)
    tgt_col = lax.shift_right_logical(jnp.broadcast_to(col_col, (nblk, nblk)), tiles.bit_length() - 1)
    same = tgt_row == tgt_col
    rank_row = jnp.sum(jnp.where(same & (sub < lane), 1.0, 0.0), axis=0, keepdims=True).astype(jnp.int32)
    rank_col = jnp.sum(jnp.where(same & (lane < sub), 1.0, 0.0), axis=1, keepdims=True).astype(jnp.int32)
    tb = tiles.bit_length() - 1
    cb = CORES.bit_length() - 1
    yb = ny.bit_length() - 1

    def place(cols, rank, kind):
        tile = cols & (tiles - 1)
        core = lax.shift_right_logical(cols, tb) & (CORES - 1)
        y = lax.shift_right_logical(cols, tb + cb) & (ny - 1)
        z = lax.shift_right_logical(cols, tb + cb + yb)
        first, second = (y, z) if kind == 0 else (z, y)
        slots = ring2[kind] * CAP
        return (first * CORES + core) * slots + second * CAP + rank, second * tiles + tile

    for kind in (0, 1):
        n1 = ring[kind] * CORES
        slots = ring2[kind] * CAP
        pos_row, _ = place(col_row, rank_row, kind)
        pos_col, id_col = place(col_col, rank_col, kind)
        slot_no = lax.broadcasted_iota(jnp.int32, (n1 * slots, nblk), 0)
        pick[kind] = jnp.where(slot_no == pos_row, 1.0, 0.0).astype(BF16)
        lane_slot = lax.broadcasted_iota(jnp.int32, (nblk, PATCH), 1) & (slots - 1)
        id_value = (id_col + 1).astype(F32)
        pos_wide = jnp.broadcast_to(pos_col, (nblk, PATCH)) - lane_slot
        for q in range(n1):
            hit = jnp.where(pos_wide == q * slots, id_value, 0.0)
            meta_send[kind, q] = jnp.sum(hit, axis=0, keepdims=True) - 1.0

    def scale(p, first):
        lo = p * bp
        for t in range(tiles):
            lanes = slice(t * PATCH, (t + 1) * PATCH)
            adj = seed_ref[lo:lo + bp, lanes]
            if not first:
                adj = adj + acc[p, pl.ds(t, bp, stride=tiles), :]
            scaled[p, t, 0:bp, :] = ((1.0 - emis_ref[0:1, lanes]) * adj).astype(BF16)

    def products(p, arriving):
        def body(step, carry):
            base = step * GROUP
            if arriving:
                view_in(step).wait()
            for j in range(0, GROUP, 2):
                k = base + j
                r0 = rows_ref[k] & (tiles - 1)
                r1 = rows_ref[k + 1] & (tiles - 1)
                left = jnp.concatenate([scaled[p, r0], scaled[p, r1]], axis=0)
                right = jnp.concatenate([view[k], view[k + 1]], axis=1)
                out = jnp.dot(left, right, preferred_element_type=F32)
                n = scaled.shape[2]
                terms[p, pl.ds(k, bp, stride=nblk), :] = out[0:bp, 0:PATCH]
                terms[p, pl.ds(k + 1, bp, stride=nblk), :] = out[n:n + bp, PATCH:2 * PATCH]
            return carry

        lax.fori_loop(0, nblk // GROUP, body, 0)

    def choose(it, p):
        for j in range(bp):
            kind, jb = divmod(j, hb)
            rows = slice(j * nblk, (j + 1) * nblk)
            value = terms[p, rows, :]
            if it == 0:
                value = value.astype(BF16)
                prev[p, rows, :] = value
            else:
                value = (value - prev[p, rows, :].astype(F32)).astype(BF16)
            n1 = ring[kind] * CORES
            slots = ring2[kind] * CAP
            out = jnp.dot(pick[kind], value, preferred_element_type=F32).astype(BF16)
            s1_send[it, p, kind, :, jb] = out.reshape(n1, slots, PATCH)
        for kind in (0, 1):
            own = mine[kind] * CORES + my_c
            s1_recv[it, p, kind, own] = s1_send[it, p, kind, own]

    def send1(it, p):
        for kind, pos, core, dev, off, dc in order1:
            pltpu.make_async_remote_copy(
                src_ref=s1_send.at[it, p, kind, pos * CORES + core],
                dst_ref=s1_recv.at[it, p, kind, mine[kind] * CORES + my_c],
                send_sem=s1_ss.at[it, p, kind], recv_sem=s1_rs.at[it, p, kind],
                device_id={"tiles": dev}, device_id_type=MESH).start()

    def wait1(it, p, kind):
        n1 = ring[kind] * CORES
        ref = s1_recv.at[it, p, kind, 0:n1 - 1]
        pltpu.make_async_copy(ref, ref, s1_rs.at[it, p, kind]).wait()

    def send_meta():
        for kind, pos, core, dev, off, dc in order1:
            pltpu.make_async_remote_copy(
                src_ref=meta_send.at[kind, pos * CORES + core],
                dst_ref=meta_recv.at[kind, mine[kind] * CORES + my_c],
                send_sem=meta_ss.at[kind], recv_sem=meta_rs.at[kind],
                device_id={"tiles": dev}, device_id_type=MESH).start()

    def take_meta(kind):
        n1 = ring[kind] * CORES
        slots = ring2[kind] * CAP
        own = mine[kind] * CORES + my_c
        ref = meta_recv.at[kind, 0:n1 - 1]
        pltpu.make_async_copy(ref, ref, meta_rs.at[kind]).wait()
        meta_recv[kind, own] = meta_send[kind, own]
        per = PATCH // slots
        rows = ring2[kind] * tiles
        part = lax.broadcasted_iota(jnp.int32, (1, PATCH), 1) // slots
        row_no = lax.broadcasted_iota(jnp.int32, (rows, PATCH), 0).astype(F32)
        for h in range(n1 // per):
            ids = jnp.zeros((1, PATCH), F32)
            for j in range(per):
                ids = jnp.where(part == j, meta_recv[kind, h * per + j], ids)
            select[kind, :, h * PATCH:(h + 1) * PATCH] = jnp.where(row_no == ids, 1.0, 0.0).astype(BF16)

    def middle(it, p, kind):
        n1 = ring[kind] * CORES
        n2 = ring2[kind]
        slots = n2 * CAP
        for jb in range(hb):
            got = s1_recv[it, p, kind, :, jb].reshape(n1 * slots, PATCH)
            total = jnp.dot(select[kind], got, preferred_element_type=F32)
            if it > 0:
                total = total + mid_rest[p, kind, jb]
            out = total.astype(BF16)
            if it < ITERS - 1:
                mid_rest[p, kind, jb] = total - out.astype(F32)
            s2_send[it, p, kind, :, jb] = out.reshape(n2, tiles, PATCH)
        own = mine2[kind]
        s2_recv[it, p, kind, own] = s2_send[it, p, kind, own]

    def send2(it, p, kinds):
        for kind, pos, dev in order2:
            if kind in kinds:
                pltpu.make_async_remote_copy(
                    src_ref=s2_send.at[it, p, kind, pos],
                    dst_ref=s2_recv.at[it, p, kind, mine2[kind]],
                    send_sem=s2_ss.at[it, p, kind], recv_sem=s2_rs.at[it, p, kind],
                    device_id={"tiles": dev}, device_id_type=MESH).start()

    def finish(it, p):
        for kind in (0, 1):
            n2 = ring2[kind]
            ref = s2_recv.at[it, p, kind, 0:n2 - 1]
            pltpu.make_async_copy(ref, ref, s2_rs.at[it, p, kind]).wait()
            for jb in range(hb):
                total = s2_recv[it, p, kind, 0, jb].astype(F32)
                for j in range(1, n2):
                    total = total + s2_recv[it, p, kind, j, jb].astype(F32)
                row = (kind * hb + jb) * tiles
                if it > 0:
                    total = total + acc[p, row:row + tiles, :]
                acc[p, row:row + tiles, :] = total

    if scaled.shape[2] > bp:
        pad = scaled.shape[2] - bp
        for p in range(PAIRS):
            scaled[p, :, bp:, :] = jnp.zeros((tiles, pad, PATCH), BF16)
    seed_in.wait()
    emis_in.wait()
    rows_in.wait()
    for it in range(ITERS):
        for p in range(PAIRS):
            if it > 0:
                finish(it - 1, p)
            scale(p, it == 0)
            products(p, it == 0 and p == 0)
            choose(it, p)
            if it == 0 and p == 0:
                pl.semaphore_wait(barrier, met)
            send1(it, p)
            if it == 0 and p == 0:
                send_meta()
        for p in range(PAIRS):
            if it == 0 and p == 0:
                take_meta(0)
                take_meta(1)
            for kind in (0, 1):
                wait1(it, p, kind)
                middle(it, p, kind)
                send2(it, p, (kind,))

    power_in.wait()
    irr_in.wait()
    for p in range(PAIRS):
        finish(ITERS - 1, p)
        lo = p * bp
        for t in range(tiles):
            lanes = slice(t * PATCH, (t + 1) * PATCH)
            adj = seed_ref[lo:lo + bp, lanes] + acc[p, pl.ds(t, bp, stride=tiles), :]
            adj_ref[lo:lo + bp, lanes] = adj
            contrast = power_ref[lo:lo + bp, lanes] - irr_ref[lo:lo + bp, lanes]
            part = jnp.sum(adj * contrast, axis=0, keepdims=True)
            if p > 0:
                part = part + g_part[t:t + 1, :]
            g_part[t:t + 1, :] = part
    for i, x in enumerate(x_peers):
        pltpu.make_async_remote_copy(
            src_ref=g_part, dst_ref=g_recv.at[i], send_sem=g_ss, recv_sem=g_rs,
            device_id={"bands": x}, device_id_type=MESH).start()
    for kind in (0, 1):
        n1 = ring[kind] * CORES
        n2 = ring2[kind]
        ref = meta_send.at[kind, 0:n1 - 1]
        pltpu.make_async_copy(ref, ref, meta_ss.at[kind]).wait()
        for it in range(ITERS):
            for p in range(PAIRS):
                ref = s1_send.at[it, p, kind, 0:n1 - 1]
                pltpu.make_async_copy(ref, ref, s1_ss.at[it, p, kind]).wait()
                ref = s2_send.at[it, p, kind, 0:n2 - 1]
                pltpu.make_async_copy(ref, ref, s2_ss.at[it, p, kind]).wait()
    pltpu.make_async_copy(g_recv, g_recv, g_rs).wait()
    total = g_part[...]
    for i in range(nx - 1):
        total = total + g_recv[i]
    grad_ref[...] = total * (1.0 / BANDS)
    pltpu.make_async_copy(g_recv, g_recv, g_ss).wait()


def hand_on(adj_ref, grad_ref, adj_out, grad_out, sems):
    copies = [pltpu.make_async_copy(adj_ref, adj_out, sems.at[0]),
              pltpu.make_async_copy(grad_ref, grad_out, sems.at[1])]
    for copy in copies:
        copy.start()
    for copy in copies:
        copy.wait()


def local(dims, view_tiles, vis_rows, vis_cols, seed_grad, emissivity, emissive_power, irradiance):
    nz, ny, nx = dims
    nblk = view_tiles.shape[0]
    bands, width = seed_grad.shape
    tiles = width // PATCH
    bp = bands // PAIRS
    hb = bp // 2
    rp = -(-bp // 8) * 8
    n1, n2 = ny * CORES, nz
    slots = n2 * CAP
    hbm = pl.BlockSpec(memory_space=pltpu.HBM)
    vmem = pl.BlockSpec(memory_space=pltpu.VMEM)
    dma = pltpu.SemaphoreType.DMA
    shapes = (jax.ShapeDtypeStruct((bands, width), F32), jax.ShapeDtypeStruct((tiles, PATCH), F32))
    results = pl.pallas_call(
        functools.partial(kernel, dims),
        out_shape=shapes,
        in_specs=[hbm] * 7,
        out_specs=(vmem, vmem),
        scratch_shapes=[
            pltpu.VMEM((nblk, PATCH, PATCH), BF16),
            pltpu.SMEM((nblk,), jnp.int32),
            pltpu.VMEM((1, nblk), jnp.int32),
            pltpu.VMEM((bands, width), F32),
            pltpu.VMEM((1, width), F32),
            pltpu.VMEM((bands, width), F32),
            pltpu.VMEM((bands, width), F32),
            pltpu.VMEM((PAIRS, tiles, rp, PATCH), BF16),
            pltpu.VMEM((PAIRS, bp * nblk, PATCH), F32),
            pltpu.VMEM((PAIRS, bp * nblk, PATCH), BF16),
            pltpu.VMEM((2, n1 * slots, nblk), BF16),
            pltpu.VMEM((2, n2 * tiles, n1 * slots), BF16),
            pltpu.VMEM((PAIRS, 2, hb, n2 * tiles, PATCH), F32),
            pltpu.VMEM((PAIRS, bp * tiles, PATCH), F32),
            pltpu.VMEM((2, n1, 1, PATCH), F32),
            pltpu.VMEM((2, n1, 1, PATCH), F32),
            pltpu.VMEM((ITERS, PAIRS, 2, n1, hb, slots, PATCH), BF16),
            pltpu.VMEM((ITERS, PAIRS, 2, n1, hb, slots, PATCH), BF16),
            pltpu.VMEM((ITERS, PAIRS, 2, n2, hb, tiles, PATCH), BF16),
            pltpu.VMEM((ITERS, PAIRS, 2, n2, hb, tiles, PATCH), BF16),
            pltpu.VMEM((tiles, PATCH), F32),
            pltpu.VMEM((nx - 1, tiles, PATCH), F32),
            dma((6,)), dma((nblk // GROUP,)),
            dma((2,)), dma((2,)),
            dma((ITERS, PAIRS, 2)), dma((ITERS, PAIRS, 2)),
            dma((ITERS, PAIRS, 2)), dma((ITERS, PAIRS, 2)),
            dma, dma,
        ],
        compiler_params=pltpu.CompilerParams(
            collective_id=0, has_side_effects=True, vmem_limit_bytes=40 * 2**20),
    )(*[pltpu.with_memory_space_constraint(x, pltpu.HBM) for x in (
        view_tiles, vis_rows, vis_cols.reshape(1, nblk), seed_grad, emissivity.reshape(1, width),
        emissive_power, irradiance)])
    adjoint, grad = results
    return adjoint, grad.reshape(width)


def solution(mesh):
    placed = (
        P("tiles", None, None),
        P("tiles"),
        P("tiles"),
        P("bands", "tiles"),
        P("tiles"),
        P("bands", "tiles"),
        P("bands", "tiles"),
    )
    side = 1
    while side * side * CORES < mesh.shape["tiles"]:
        side *= 2
    dims = (mesh.shape["tiles"] // (CORES * side), side, mesh.shape["bands"])
    return jax.shard_map(
        functools.partial(local, dims),
        mesh=mesh,
        in_specs=placed,
        out_specs=(P("bands", "tiles"), P("tiles")),
        check_vma=False,
    )
```

```python
import functools

import jax
import jax.numpy as jnp
from jax import lax
from jax.experimental import pallas as pl
from jax.experimental.pallas import tpu as pltpu
from jax.sharding import PartitionSpec as P

BANDS = 48
ITERS = 2
PATCH = 128
CAP = 2
CORES = 2
PAIRS = 3
GROUP = 24
F32, BF16 = jnp.float32, jnp.bfloat16
ORDER = (("s", 0), ("s", 1), ("s", 2), ("m", 0), ("m", 1), ("m", 2), ("s", 3), ("s", 4), ("s", 5), ("m", 3), ("m", 4), ("m", 5))
MESH = pl.DeviceIdType.MESH


def far_first(n):
    out = []
    for d in range(n // 2, 0, -1):
        out.append(d)
        if n - d != d:
            out.append(n - d)
    return out


def kernel(dims, *refs):
    nz, ny, nx = dims
    (view_hbm, rows_hbm, cols_hbm, seed_hbm, emis_hbm, power_hbm, irr_hbm,
     adj_ref, grad_ref,
     view, rows_ref, cols_ref, seed_ref, emis_ref, power_ref, irr_ref,
     scaled, terms, prev, pick, select, mid_rest, acc,
     meta_send, meta_recv, s1_send, s1_recv, s2_send, s2_recv, g_part, g_recv,
     in_sems, view_sems, meta_ss, meta_rs, s1_ss, s1_rs, s2_ss, s2_rs, g_ss, g_rs) = refs
    nblk = view.shape[0]
    bands, width = seed_ref.shape
    tiles = width // PATCH
    bp = bands // PAIRS
    hb = bp // 2
    me = lax.axis_index("tiles")
    my_x = lax.axis_index("bands")
    my_c = lax.rem(me, CORES)
    my_y = lax.rem(me // CORES, ny)
    my_z = me // (CORES * ny)
    ring = (ny, nz)
    ring2 = (nz, ny)
    mine = (my_y, my_z)
    mine2 = (my_z, my_y)

    def index_of(kind, first, second, core):
        y, z = (first, second) if kind == 0 else (second, first)
        return (z * ny + y) * CORES + core

    peers1, peers2 = [], []
    for kind in (0, 1):
        p1, p2 = [], []
        for off in far_first(ring[kind]) + [0]:
            for dc in (1, 0):
                if off == 0 and dc == 0:
                    continue
                pos = lax.rem(mine[kind] + off, ring[kind])
                core = lax.rem(my_c + dc, CORES)
                p1.append((kind, pos, core, index_of(kind, pos, mine2[kind], core), off, dc))
        for off in far_first(ring2[kind]):
            pos = lax.rem(mine2[kind] + off, ring2[kind])
            p2.append((kind, pos, index_of(kind, mine[kind], pos, my_c)))
        peers1.append(p1)
        peers2.append(p2)

    def interleave(a, b):
        out = []
        for i in range(max(len(a), len(b))):
            out += a[i:i + 1] + b[i:i + 1]
        return out

    order1 = interleave(*peers1)
    order2 = interleave(*peers2)
    x_peers = [lax.rem(my_x + off, nx) for off in range(1, nx)]

    cols_in, rows_in, seed_in, emis_in, power_in, irr_in = [
        pltpu.make_async_copy(src, dst, in_sems.at[i]) for i, (src, dst) in enumerate((
            (cols_hbm, cols_ref), (rows_hbm, rows_ref), (seed_hbm, seed_ref), (emis_hbm, emis_ref),
            (power_hbm, power_ref), (irr_hbm, irr_ref)))]

    def view_in(step):
        part = pl.ds(step * GROUP, GROUP)
        return pltpu.make_async_copy(view_hbm.at[part], view.at[part], view_sems.at[step])

    for copy in (cols_in, rows_in, seed_in, emis_in):
        copy.start()
    for step in range(nblk // GROUP):
        view_in(step).start()
    power_in.start()
    irr_in.start()
    barrier = pltpu.get_barrier_semaphore()
    met = 0
    for kind, pos, core, dev, off, dc in order1:
        if kind == 1 and off == 0:
            continue
        pl.semaphore_signal(barrier, inc=1, device_id={"tiles": dev}, device_id_type=MESH)
        met += 1
    for x in x_peers:
        pl.semaphore_signal(barrier, inc=1, device_id={"bands": x}, device_id_type=MESH)
        met += 1

    cols_in.wait()
    col_row = cols_ref[...]
    lane = lax.broadcasted_iota(jnp.int32, (nblk, nblk), 1)
    sub = lax.broadcasted_iota(jnp.int32, (nblk, nblk), 0)
    spread = jnp.broadcast_to(col_row, (nblk, nblk))
    col_col = jnp.sum(jnp.where(lane == sub, spread, 0).astype(F32), axis=1, keepdims=True).astype(jnp.int32)
    tgt_row = lax.shift_right_logical(spread, tiles.bit_length() - 1)
    tgt_col = lax.shift_right_logical(jnp.broadcast_to(col_col, (nblk, nblk)), tiles.bit_length() - 1)
    same = tgt_row == tgt_col
    rank_row = jnp.sum(jnp.where(same & (sub < lane), 1.0, 0.0), axis=0, keepdims=True).astype(jnp.int32)
    rank_col = jnp.sum(jnp.where(same & (lane < sub), 1.0, 0.0), axis=1, keepdims=True).astype(jnp.int32)
    tb = tiles.bit_length() - 1
    cb = CORES.bit_length() - 1
    yb = ny.bit_length() - 1

    def place(cols, rank, kind):
        tile = cols & (tiles - 1)
        core = lax.shift_right_logical(cols, tb) & (CORES - 1)
        y = lax.shift_right_logical(cols, tb + cb) & (ny - 1)
        z = lax.shift_right_logical(cols, tb + cb + yb)
        first, second = (y, z) if kind == 0 else (z, y)
        slots = ring2[kind] * CAP
        return (first * CORES + core) * slots + second * CAP + rank, second * tiles + tile

    placed = []
    for kind in (0, 1):
        n1 = ring[kind] * CORES
        slots = ring2[kind] * CAP
        pos_row, _ = place(col_row, rank_row, kind)
        pos_col, id_col = place(col_col, rank_col, kind)
        slot_no = lax.broadcasted_iota(jnp.int32, (n1 * slots, nblk), 0)
        pick[kind] = jnp.where(slot_no == pos_row, 1.0, 0.0).astype(BF16)
        placed.append((pos_col, id_col))

    def scale(p, first):
        lo = p * bp
        for t in range(tiles):
            lanes = slice(t * PATCH, (t + 1) * PATCH)
            adj = seed_ref[lo:lo + bp, lanes]
            if not first:
                adj = adj + acc[p, pl.ds(t, bp, stride=tiles), :]
            scaled[p, t, 0:bp, :] = ((1.0 - emis_ref[0:1, lanes]) * adj).astype(BF16)

    def products(p, arriving):
        def body(step, carry):
            base = step * GROUP
            if arriving:
                view_in(step).wait()
            for j in range(0, GROUP, 2):
                k = base + j
                r0 = rows_ref[k] & (tiles - 1)
                r1 = rows_ref[k + 1] & (tiles - 1)
                left = jnp.concatenate([scaled[p, r0], scaled[p, r1]], axis=0)
                right = jnp.concatenate([view[k], view[k + 1]], axis=1)
                out = jnp.dot(left, right, preferred_element_type=F32)
                n = scaled.shape[2]
                terms[p, pl.ds(k, bp, stride=nblk), :] = out[0:bp, 0:PATCH]
                terms[p, pl.ds(k + 1, bp, stride=nblk), :] = out[n:n + bp, PATCH:2 * PATCH]
            return carry

        lax.fori_loop(0, nblk // GROUP, body, 0)

    def choose(it, p):
        for j in range(bp):
            kind, jb = divmod(j, hb)
            rows = slice(j * nblk, (j + 1) * nblk)
            value = terms[p, rows, :]
            if it == 0:
                value = value.astype(BF16)
                prev[p, rows, :] = value
            else:
                value = (value - prev[p, rows, :].astype(F32)).astype(BF16)
            n1 = ring[kind] * CORES
            slots = ring2[kind] * CAP
            out = jnp.dot(pick[kind], value, preferred_element_type=F32).astype(BF16)
            s1_send[it, p, kind, :, jb] = out.reshape(n1, slots, PATCH)
        for kind in (0, 1):
            own = mine[kind] * CORES + my_c
            s1_recv[it, p, kind, own] = s1_send[it, p, kind, own]

    def send1(it, p):
        for kind, pos, core, dev, off, dc in order1:
            pltpu.make_async_remote_copy(
                src_ref=s1_send.at[it, p, kind, pos * CORES + core],
                dst_ref=s1_recv.at[it, p, kind, mine[kind] * CORES + my_c],
                send_sem=s1_ss.at[it, p, kind], recv_sem=s1_rs.at[it, p, kind],
                device_id={"tiles": dev}, device_id_type=MESH).start()

    def wait1(it, p, kind):
        n1 = ring[kind] * CORES
        ref = s1_recv.at[it, p, kind, 0:n1 - 1]
        pltpu.make_async_copy(ref, ref, s1_rs.at[it, p, kind]).wait()

    def send_meta():
        for kind, (pos_col, id_col) in enumerate(placed):
            n1 = ring[kind] * CORES
            slots = ring2[kind] * CAP
            lane_slot = lax.broadcasted_iota(jnp.int32, (nblk, PATCH), 1) & (slots - 1)
            id_value = (id_col + 1).astype(F32)
            pos_wide = jnp.broadcast_to(pos_col, (nblk, PATCH)) - lane_slot
            for q in range(n1):
                hit = jnp.where(pos_wide == q * slots, id_value, 0.0)
                meta_send[kind, q] = jnp.sum(hit, axis=0, keepdims=True) - 1.0
        for kind, pos, core, dev, off, dc in order1:
            pltpu.make_async_remote_copy(
                src_ref=meta_send.at[kind, pos * CORES + core],
                dst_ref=meta_recv.at[kind, mine[kind] * CORES + my_c],
                send_sem=meta_ss.at[kind], recv_sem=meta_rs.at[kind],
                device_id={"tiles": dev}, device_id_type=MESH).start()

    def take_meta(kind):
        n1 = ring[kind] * CORES
        slots = ring2[kind] * CAP
        own = mine[kind] * CORES + my_c
        ref = meta_recv.at[kind, 0:n1 - 1]
        pltpu.make_async_copy(ref, ref, meta_rs.at[kind]).wait()
        meta_recv[kind, own] = meta_send[kind, own]
        per = PATCH // slots
        rows = ring2[kind] * tiles
        part = lax.broadcasted_iota(jnp.int32, (1, PATCH), 1) // slots
        row_no = lax.broadcasted_iota(jnp.int32, (rows, PATCH), 0).astype(F32)
        for h in range(n1 // per):
            ids = jnp.zeros((1, PATCH), F32)
            for j in range(per):
                ids = jnp.where(part == j, meta_recv[kind, h * per + j], ids)
            select[kind, :, h * PATCH:(h + 1) * PATCH] = jnp.where(row_no == ids, 1.0, 0.0).astype(BF16)

    def middle(it, p, kind):
        n1 = ring[kind] * CORES
        n2 = ring2[kind]
        slots = n2 * CAP
        for jb in range(hb):
            got = s1_recv[it, p, kind, :, jb].reshape(n1 * slots, PATCH)
            total = jnp.dot(select[kind], got, preferred_element_type=F32)
            if it > 0:
                total = total + mid_rest[p, kind, jb]
            out = total.astype(BF16)
            if it < ITERS - 1:
                mid_rest[p, kind, jb] = total - out.astype(F32)
            s2_send[it, p, kind, :, jb] = out.reshape(n2, tiles, PATCH)
        own = mine2[kind]
        s2_recv[it, p, kind, own] = s2_send[it, p, kind, own]

    def send2(it, p, kinds):
        for kind, pos, dev in order2:
            if kind in kinds:
                pltpu.make_async_remote_copy(
                    src_ref=s2_send.at[it, p, kind, pos],
                    dst_ref=s2_recv.at[it, p, kind, mine2[kind]],
                    send_sem=s2_ss.at[it, p, kind], recv_sem=s2_rs.at[it, p, kind],
                    device_id={"tiles": dev}, device_id_type=MESH).start()

    def finish(it, p):
        for kind in (0, 1):
            n2 = ring2[kind]
            ref = s2_recv.at[it, p, kind, 0:n2 - 1]
            pltpu.make_async_copy(ref, ref, s2_rs.at[it, p, kind]).wait()
            for jb in range(hb):
                total = s2_recv[it, p, kind, 0, jb].astype(F32)
                for j in range(1, n2):
                    total = total + s2_recv[it, p, kind, j, jb].astype(F32)
                row = (kind * hb + jb) * tiles
                if it > 0:
                    total = total + acc[p, row:row + tiles, :]
                acc[p, row:row + tiles, :] = total

    if scaled.shape[2] > bp:
        pad = scaled.shape[2] - bp
        for p in range(PAIRS):
            scaled[p, :, bp:, :] = jnp.zeros((tiles, pad, PATCH), BF16)
    seed_in.wait()
    emis_in.wait()
    rows_in.wait()
    def sweep(it, p):
        if it > 0:
            finish(it - 1, p)
        scale(p, it == 0)
        products(p, it == 0 and p == 0)
        choose(it, p)
        if it == 0 and p == 0:
            pl.semaphore_wait(barrier, met)
        send1(it, p)
        if it == 0 and p == 0:
            send_meta()

    def turn(it, p):
        if it == 0 and p == 0:
            take_meta(0)
            take_meta(1)
        for kind in (0, 1):
            wait1(it, p, kind)
            middle(it, p, kind)
            send2(it, p, (kind,))

    for what, step in ORDER:
        (sweep if what == "s" else turn)(*divmod(step, PAIRS))

    power_in.wait()
    irr_in.wait()
    for p in range(PAIRS):
        finish(ITERS - 1, p)
        lo = p * bp
        for t in range(tiles):
            lanes = slice(t * PATCH, (t + 1) * PATCH)
            adj = seed_ref[lo:lo + bp, lanes] + acc[p, pl.ds(t, bp, stride=tiles), :]
            adj_ref[lo:lo + bp, lanes] = adj
            contrast = power_ref[lo:lo + bp, lanes] - irr_ref[lo:lo + bp, lanes]
            part = jnp.sum(adj * contrast, axis=0, keepdims=True)
            if p > 0:
                part = part + g_part[t:t + 1, :]
            g_part[t:t + 1, :] = part
    for i, x in enumerate(x_peers):
        pltpu.make_async_remote_copy(
            src_ref=g_part, dst_ref=g_recv.at[i], send_sem=g_ss, recv_sem=g_rs,
            device_id={"bands": x}, device_id_type=MESH).start()
    for kind in (0, 1):
        n1 = ring[kind] * CORES
        n2 = ring2[kind]
        ref = meta_send.at[kind, 0:n1 - 1]
        pltpu.make_async_copy(ref, ref, meta_ss.at[kind]).wait()
        for it in range(ITERS):
            for p in range(PAIRS):
                ref = s1_send.at[it, p, kind, 0:n1 - 1]
                pltpu.make_async_copy(ref, ref, s1_ss.at[it, p, kind]).wait()
                ref = s2_send.at[it, p, kind, 0:n2 - 1]
                pltpu.make_async_copy(ref, ref, s2_ss.at[it, p, kind]).wait()
    pltpu.make_async_copy(g_recv, g_recv, g_rs).wait()
    total = g_part[...]
    for i in range(nx - 1):
        total = total + g_recv[i]
    grad_ref[...] = total * (1.0 / BANDS)
    pltpu.make_async_copy(g_recv, g_recv, g_ss).wait()


def hand_on(adj_ref, grad_ref, adj_out, grad_out, sems):
    copies = [pltpu.make_async_copy(adj_ref, adj_out, sems.at[0]),
              pltpu.make_async_copy(grad_ref, grad_out, sems.at[1])]
    for copy in copies:
        copy.start()
    for copy in copies:
        copy.wait()


def local(dims, view_tiles, vis_rows, vis_cols, seed_grad, emissivity, emissive_power, irradiance):
    nz, ny, nx = dims
    nblk = view_tiles.shape[0]
    bands, width = seed_grad.shape
    tiles = width // PATCH
    bp = bands // PAIRS
    hb = bp // 2
    rp = -(-bp // 8) * 8
    n1, n2 = ny * CORES, nz
    slots = n2 * CAP
    hbm = pl.BlockSpec(memory_space=pltpu.HBM)
    vmem = pl.BlockSpec(memory_space=pltpu.VMEM)
    dma = pltpu.SemaphoreType.DMA
    shapes = (jax.ShapeDtypeStruct((bands, width), F32), jax.ShapeDtypeStruct((tiles, PATCH), F32))
    results = pl.pallas_call(
        functools.partial(kernel, dims),
        out_shape=shapes,
        in_specs=[hbm] * 7,
        out_specs=(vmem, vmem),
        scratch_shapes=[
            pltpu.VMEM((nblk, PATCH, PATCH), BF16),
            pltpu.SMEM((nblk,), jnp.int32),
            pltpu.VMEM((1, nblk), jnp.int32),
            pltpu.VMEM((bands, width), F32),
            pltpu.VMEM((1, width), F32),
            pltpu.VMEM((bands, width), F32),
            pltpu.VMEM((bands, width), F32),
            pltpu.VMEM((PAIRS, tiles, rp, PATCH), BF16),
            pltpu.VMEM((PAIRS, bp * nblk, PATCH), F32),
            pltpu.VMEM((PAIRS, bp * nblk, PATCH), BF16),
            pltpu.VMEM((2, n1 * slots, nblk), BF16),
            pltpu.VMEM((2, n2 * tiles, n1 * slots), BF16),
            pltpu.VMEM((PAIRS, 2, hb, n2 * tiles, PATCH), F32),
            pltpu.VMEM((PAIRS, bp * tiles, PATCH), F32),
            pltpu.VMEM((2, n1, 1, PATCH), F32),
            pltpu.VMEM((2, n1, 1, PATCH), F32),
            pltpu.VMEM((ITERS, PAIRS, 2, n1, hb, slots, PATCH), BF16),
            pltpu.VMEM((ITERS, PAIRS, 2, n1, hb, slots, PATCH), BF16),
            pltpu.VMEM((ITERS, PAIRS, 2, n2, hb, tiles, PATCH), BF16),
            pltpu.VMEM((ITERS, PAIRS, 2, n2, hb, tiles, PATCH), BF16),
            pltpu.VMEM((tiles, PATCH), F32),
            pltpu.VMEM((nx - 1, tiles, PATCH), F32),
            dma((6,)), dma((nblk // GROUP,)),
            dma((2,)), dma((2,)),
            dma((ITERS, PAIRS, 2)), dma((ITERS, PAIRS, 2)),
            dma((ITERS, PAIRS, 2)), dma((ITERS, PAIRS, 2)),
            dma, dma,
        ],
        compiler_params=pltpu.CompilerParams(
            collective_id=0, has_side_effects=True, vmem_limit_bytes=40 * 2**20),
    )(*[pltpu.with_memory_space_constraint(x, pltpu.HBM) for x in (
        view_tiles, vis_rows, vis_cols.reshape(1, nblk), seed_grad, emissivity.reshape(1, width),
        emissive_power, irradiance)])
    adjoint, grad = pl.pallas_call(
        hand_on,
        out_shape=shapes,
        in_specs=[vmem] * 2,
        out_specs=(hbm, hbm),
        scratch_shapes=[dma((2,))],
    )(*[pltpu.with_memory_space_constraint(x, pltpu.VMEM) for x in results])
    return adjoint, grad.reshape(width)


def solution(mesh):
    placed = (
        P("tiles", None, None),
        P("tiles"),
        P("tiles"),
        P("bands", "tiles"),
        P("tiles"),
        P("bands", "tiles"),
        P("bands", "tiles"),
    )
    side = 1
    while side * side * CORES < mesh.shape["tiles"]:
        side *= 2
    dims = (mesh.shape["tiles"] // (CORES * side), side, mesh.shape["bands"])
    return jax.shard_map(
        functools.partial(local, dims),
        mesh=mesh,
        in_specs=placed,
        out_specs=(P("bands", "tiles"), P("tiles")),
        check_vma=False,
    )
```
